256 devices in a mesh: section: 8 (over z_hi, x), tp: 32 (over z_lo, y, core).
Axes of the slice: x: 4, y: 4, z: 8 (z_hi: 2, z_lo: 4; z = z_hi * 4 + z_lo), core: 2. Of those that a mesh axis runs over, the one named last changes fastest.
Arguments:
- fresh_in: bfloat16 [128, 12288], P(None, 'tp'), may hold values from -25 to 25
- fwd_in: bfloat16 [8, 128, 12288], P('section', None, 'tp'), may hold values from -25 to 25
- fresh_cot: bfloat16 [128, 12288], P(None, 'tp'), may hold values from -7 to 7
- cot_in: bfloat16 [8, 128, 12288], P('section', None, 'tp'), may hold values from -7 to 7
- stash_in: bfloat16 [8, 2, 128, 12288], P('section', None, None, 'tp'), may hold values from -25 to 25
- weight: bfloat16 [8, 12288, 12288], P('section', None, 'tp'), may hold values from -0.0546875 to 0.0546875
- gain: float32 [8, 12288], P('section'), may hold values from 0.25 to 1.75
Outputs:
- first_out: bfloat16 [8, 128, 12288], P('section', None, 'tp')
- second_out: bfloat16 [8, 128, 12288], P('section', None, 'tp')
- first_grad: bfloat16 [8, 128, 12288], P('section', None, 'tp')
- second_grad: bfloat16 [8, 128, 12288], P('section', None, 'tp')
- stash_out: bfloat16 [8, 2, 128, 12288], P('section', None, None, 'tp')
The draws below stay inside these ranges and needn't reach their ends.
All inputs are finite; a program needn't handle non-finite values.
Results may differ from the reference program's by a relative error of at most 0.019.
Values may be sent and summed in bfloat16 or wider, within the bound.
A program may use at most 64 MiB of HBM per device.

```python
import jax
import jax.numpy as jnp
from jax import lax

D = 12288
TOK = 128
SECTIONS = 8
N_TP = 32


def column_ramp(key, width):
    col = jnp.arange(width, dtype=jnp.float32)
    return (1.0 + 2.0 * col / width) * jnp.exp(jax.random.uniform(key, (width,), jnp.float32, 0.0, 0.7)) / 2.0


def scaled_rows(key, noise):
    k_rows, k_cols = jax.random.split(key)
    rows_scale = jnp.exp(jax.random.uniform(k_rows, noise.shape[:-1] + (1,), jnp.float32, 0.0, 0.7))
    return (noise * rows_scale * column_ramp(k_cols, noise.shape[-1])).astype(jnp.bfloat16)


def level_field(key, shape):
    k_rows, k_cols = jax.random.split(key)
    rows_level = jnp.exp(jax.random.uniform(k_rows, shape[:-1] + (1,), jnp.float32, -0.51, 0.47))
    cols_level = jnp.exp(jax.random.uniform(k_cols, (shape[-1],), jnp.float32, 0.0, 0.5))
    return rows_level * cols_level


def draw_fresh_in(key, part):
    key = jax.random.fold_in(key, 11)
    k_noise, k_scale = jax.random.split(key)
    noise = jax.random.truncated_normal(k_noise, -4.0, 4.0, (TOK, D), jnp.float32)
    return scaled_rows(k_scale, noise)


def draw_fwd_in(key, part):
    key = jax.random.fold_in(key, 23)
    k_noise, k_scale = jax.random.split(key)
    noise = jax.random.truncated_normal(k_noise, -4.0, 4.0, (SECTIONS, TOK, D), jnp.float32)
    return scaled_rows(k_scale, noise)


def draw_stash_in(key, part):
    key = jax.random.fold_in(key, 37)
    k_noise, k_scale = jax.random.split(key)
    noise = jax.random.truncated_normal(k_noise, -4.0, 4.0, (SECTIONS, 2, TOK, D), jnp.float32)
    return scaled_rows(k_scale, noise)


def draw_cot_in(key, part):
    key = jax.random.fold_in(key, 41)
    k_noise, k_level = jax.random.split(key)
    noise = jax.random.truncated_normal(k_noise, -4.0, 4.0, (SECTIONS, TOK, D), jnp.float32)
    level = level_field(k_level, (SECTIONS, TOK, D))
    return (noise + level).astype(jnp.bfloat16)


def draw_fresh_cot(key, part):
    key = jax.random.fold_in(key, 53)
    k_noise, k_level = jax.random.split(key)
    noise = jax.random.truncated_normal(k_noise, -4.0, 4.0, (TOK, D), jnp.float32)
    level = level_field(k_level, (TOK, D))
    return (noise + level).astype(jnp.bfloat16)


def steps_of(own_key, shape, pieces, low, largest):
    def one(axis_at, parts):
        draws = jax.random.uniform(jax.random.fold_in(jax.random.fold_in(own_key, 6), axis_at), (parts,), jnp.float32, low / len(pieces), largest / len(pieces))
        return jnp.repeat(jnp.exp(draws), shape[axis_at] // parts).reshape((-1,) + (1,) * (len(shape) - axis_at - 1))

    level = one(*pieces[0])
    for cut in pieces[1:]:
        level = level * one(*cut)
    return level


def scatter_about(stream_key, shape, scale, reach, pieces=(), held_as=jnp.bfloat16):
    values = scale * jax.random.normal(stream_key, shape, jnp.float32)
    if pieces:
        values = values * steps_of(stream_key, shape, pieces, -0.22, 0.18)
    return jnp.clip(values, -reach, reach).astype(held_as)


def setup_inputs(seed: int = 0) -> dict:
    arg_keys = jax.random.split(jax.random.key(seed), 8)
    fresh_in = draw_fresh_in(jax.random.fold_in(arg_keys[7], 71), 0)
    fwd_in = draw_fwd_in(jax.random.fold_in(arg_keys[7], 71), 0)
    fresh_cot = draw_fresh_cot(jax.random.fold_in(arg_keys[7], 71), 0)
    cot_in = draw_cot_in(jax.random.fold_in(arg_keys[7], 71), 0)
    stash_in = draw_stash_in(jax.random.fold_in(arg_keys[7], 71), 0)
    weight = scatter_about(arg_keys[5], (SECTIONS, D, D), D ** -0.5, 0.0546875, ((0, 8), (2, 32)))
    gain = jnp.clip(1.0 + 0.15 * jax.random.normal(arg_keys[6], (SECTIONS, D), jnp.float32), 0.25, 1.75)
    return {"fresh_in": fresh_in, "fwd_in": fwd_in, "fresh_cot": fresh_cot, "cot_in": cot_in, "stash_in": stash_in, "weight": weight, "gain": gain}


EPS = 1e-05
GCOEF = 0.7978845608028654

def gelu_value(h):
    return 0.5 * h * (1.0 + jnp.tanh(GCOEF * (h + 0.044715 * h * h * h)))

def gelu_slope(h):
    tval = jnp.tanh(GCOEF * (h + 0.044715 * h * h * h))
    return 0.5 * (1.0 + tval) + 0.5 * h * (1.0 - tval * tval) * GCOEF * (1.0 + 3.0 * 0.044715 * h * h)

def layer_parts(x, w, g):
    xf = x.astype(jnp.float32)
    radius = jnp.sqrt(lax.optimization_barrier(jnp.mean(xf * xf, axis=-1, keepdims=True)) + EPS)
    normed = (g[None, :] * xf / radius).astype(jnp.bfloat16)
    hidden = jnp.dot(normed, w, preferred_element_type=jnp.float32)
    return (xf, radius, hidden)

def forward(x, w, g):
    xf, radius, hidden = layer_parts(x, w, g)
    return (xf + gelu_value(hidden)).astype(jnp.bfloat16)

def backward(x, cot, w, g):
    xf, radius, hidden = layer_parts(x, w, g)
    upstream = (cot.astype(jnp.float32) * gelu_slope(hidden)).astype(jnp.bfloat16)
    width = w.shape[0]
    blocks = width // N_TP
    u_blocks = upstream.reshape(upstream.shape[0], N_TP, blocks)
    w_blocks = w.reshape(width, N_TP, blocks)

    def add_block(total, index):
        u_part = lax.dynamic_index_in_dim(u_blocks, index, 1, keepdims=False)
        w_part = lax.dynamic_index_in_dim(w_blocks, index, 1, keepdims=False)
        partial_sum = lax.dot_general(u_part, w_part, (((1,), (1,)), ((), ())), preferred_element_type=jnp.float32)
        return (total + partial_sum.astype(jnp.bfloat16).astype(jnp.float32), None)
    start = jnp.zeros((upstream.shape[0], width), jnp.float32)
    dnorm, _ = lax.scan(add_block, start, jnp.arange(N_TP, dtype=jnp.int32))
    inner = lax.optimization_barrier(jnp.sum(dnorm * g[None, :] * xf, axis=-1, keepdims=True))
    grad = cot.astype(jnp.float32) + g[None, :] * dnorm / radius - xf * inner / (width * radius ** 3)
    return grad.astype(jnp.bfloat16)

def reference(fresh_in, fwd_in, fresh_cot, cot_in, stash_in, weight, gain):
    first_out = []
    for s in range(SECTIONS):
        first_out.append(forward(fwd_in[s], weight[s], gain[s]))
    second_in = [fresh_in] + [first_out[s - 1] for s in range(1, SECTIONS)]
    second_out = [forward(second_in[s], weight[s], gain[s]) for s in range(SECTIONS)]
    first_grad = []
    for s in range(SECTIONS):
        first_grad.append(backward(stash_in[SECTIONS - 1 - s, 0], cot_in[s], weight[s], gain[s]))
    second_cot = [first_grad[s + 1] for s in range(SECTIONS - 1)] + [fresh_cot]
    second_grad = [backward(stash_in[SECTIONS - 1 - s, 1], second_cot[s], weight[s], gain[s]) for s in range(SECTIONS)]
    stash_out = jnp.stack([jnp.stack([fwd_in[SECTIONS - 1 - j], second_in[SECTIONS - 1 - j]]) for j in range(SECTIONS)])
    return (jnp.stack(first_out), jnp.stack(second_out), jnp.stack(first_grad), jnp.stack(second_grad), stash_out)
```

```python
import functools

import jax
import jax.numpy as jnp
from jax import lax
from jax.experimental import pallas as pl
from jax.experimental.pallas import tpu as pltpu
from jax.sharding import PartitionSpec as P

EPS = 1e-05
GCOEF = 0.7978845608028654
MESH = pl.DeviceIdType.MESH

TOK = 128
W = 384
NZ = 4
NY = 4
HALF = TOK // 2
A, B, C, D = 0, 1, 2, 3
BF = jnp.bfloat16
F32 = jnp.float32


def gelu_value(h):
    return 0.5 * h * (1.0 + jnp.tanh(GCOEF * (h + 0.044715 * h * h * h)))


def gelu_slope(h):
    tval = jnp.tanh(GCOEF * (h + 0.044715 * h * h * h))
    return 0.5 * (1.0 + tval) + 0.5 * h * (1.0 - tval * tval) * GCOEF * (
        1.0 + 3.0 * 0.044715 * h * h
    )


def kernel(
    nsec,
    fresh_in, fwd_in, fresh_cot, cot_in, stash_in, weight, gain,
    first_out, second_out, first_grad, second_grad, stash_out,
    xg, wc, gv, acc, hr, uu, cot, outb, rb,
    hsend, hin, fsend, fin, zsend, zin, dnacc, qown, qc, qy, qz, qsum,
    s_z, r_z, s_y, r_y, s_r, r_r,
    s_w, r_w, l_w,
    s_h, r_h, s_u, r_u,
    s_ev, r_ev, s_next, r_next, s_prev, r_prev, s_st, r_st,
    l_in, l_out,
    s_a, r_a, s_b, r_b, s_c, r_c,
    s_q, r_q,
):
    sec = lax.axis_index("section")
    tp = lax.axis_index("tp")
    core = lax.rem(tp, 2)
    y = lax.rem(tp // 2, NY)
    z = tp // (2 * NY)
    width = NZ * NY * 2 * W

    def at(zz, yy, cc=None):
        return (sec, (zz * NY + yy) * 2 + (core if cc is None else cc))

    def turn(v, k, n):
        return lax.rem(v + k, n)

    yr, yl, yo = turn(y, 1, NY), turn(y, 3, NY), turn(y, 2, NY)
    right, left, over = at(z, yr), at(z, yl), at(z, yo)
    twin = at(z, y, 1 - core)
    mirror = (nsec - 1 - sec, tp)
    after = (turn(sec, 1, nsec), tp)
    before = (turn(sec, nsec - 1, nsec), tp)

    def far(src, dst, ssem, rsem, dev):
        return pltpu.make_async_remote_copy(
            src_ref=src, dst_ref=dst, send_sem=ssem, recv_sem=rsem,
            device_id=dev, device_id_type=MESH,
        )

    def arrived(dst, ssem, rsem):
        far(dst, dst, ssem, rsem, twin).wait_recv()

    def sent(src, ssem, rsem):
        far(src, src, ssem, rsem, twin).wait_send()

    def near(src, dst, sem):
        return pltpu.make_async_copy(src, dst, sem)

    barrier = pltpu.get_barrier_semaphore()

    def greet(dev):
        pl.semaphore_signal(barrier, inc=1, device_id=dev, device_id_type=MESH)

    for k in range(1, NZ):
        greet(at(turn(z, k, NZ), y))
    for dev in (right, left, over, twin, mirror, after, before):
        greet(dev)
    pl.semaphore_wait(barrier, 10)

    def own_sends(g, src):
        for k in range(1, NZ):
            far(src, xg.at[g, y, z], s_z.at[g, k], r_z.at[g, z],
                at(turn(z, k, NZ), y)).start()
        far(src, xg.at[g, y, z], s_y.at[g, z, 0], r_y.at[g, z, 0], right).start()
        far(src, xg.at[g, y, z], s_y.at[g, z, 1], r_y.at[g, z, 1], left).start()

    def column_sends(g):
        def body(i, carry):
            zq = turn(z, i, NZ)
            slot = xg.at[g, y, zq]
            arrived(slot, s_z.at[g, 0], r_z.at[g, zq])
            far(slot, slot, s_y.at[g, zq, 0], r_y.at[g, zq, 0], right).start()
            far(slot, slot, s_y.at[g, zq, 1], r_y.at[g, zq, 1], left).start()
            return carry
        lax.fori_loop(1, NZ, body, 0)

    def product(g, yy, zq):
        x = xg[g, yy, zq].astype(F32)
        x2 = x * x
        acc[g, :, 2 * W:] += x2[:, :128] + x2[:, 128:256] + x2[:, 256:]
        start = pl.multiple_of(((zq * NY + yy) * 2 + core) * W, 128)
        n = (x * gv[:, pl.ds(start, W)]).astype(BF)
        acc[g, :, :2 * W] += jnp.dot(n, wc[yy, zq], preferred_element_type=F32)

    def relay(g):
        def body(i, carry):
            zq = turn(z, i, NZ)
            from_left, from_right = xg.at[g, yl, zq], xg.at[g, yr, zq]
            product(g, y, zq)
            arrived(from_left, s_z.at[g, 0], r_y.at[g, zq, 0])
            top = from_left.at[pl.ds(0, HALF)]
            far(top, top, s_r.at[g, zq, 0], r_r.at[g, zq, 0], right).start()
            arrived(from_right, s_z.at[g, 0], r_y.at[g, zq, 1])
            low = from_right.at[pl.ds(HALF, HALF)]
            far(low, low, s_r.at[g, zq, 1], r_r.at[g, zq, 1], left).start()
            product(g, yl, zq)
            product(g, yr, zq)
            return carry
        lax.fori_loop(0, NZ, body, 0)

    def last_quarter(g):
        def body(i, carry):
            zq = turn(z, i, NZ)
            slot = xg.at[g, yo, zq]
            arrived(slot.at[pl.ds(0, HALF)], s_z.at[g, 0], r_r.at[g, zq, 0])
            arrived(slot.at[pl.ds(HALF, HALF)], s_z.at[g, 0], r_r.at[g, zq, 1])
            product(g, yo, zq)
            return carry
        lax.fori_loop(0, NZ, body, 0)
        far(acc.at[g, :, pl.ds(W, W + 128)], hr.at[g], s_h.at[g], r_h.at[g], twin).start()

    def hidden(g):
        arrived(hr.at[g], s_z.at[g, 0], r_h.at[g])
        ss = acc[g, :, 2 * W:] + hr[g, :, W:]
        radius = jnp.sqrt(jnp.sum(ss, axis=-1, keepdims=True) / width + EPS)
        h = (acc[g, :, :W] + hr[g, :, :W]) / radius
        return radius, h

    def part(b, yy, zq):
        return lax.dot_general(
            uu[b], wc[yy, zq], (((1,), (1,)), ((), ())), preferred_element_type=F32
        )

    def gradient_start(b, g):
        radius, h = hidden(g)
        u = (cot[b].astype(F32) * gelu_slope(h)).astype(BF)
        uu[b, :, :W] = u
        far(uu.at[b, :, pl.ds(0, W)], uu.at[b, :, pl.ds(W, W)], s_u.at[b], r_u.at[b], twin).start()
        rb[b] = jnp.broadcast_to(radius, (TOK, 128))
        e = u.astype(F32) * h
        lanes = (e[:, :128] + e[:, 128:256] + e[:, 256:]) * radius
        t = lanes.T
        q = t[0:8]
        for k in range(1, 16):
            q = q + t[8 * k:8 * k + 8]
        qown[b] = q
        far(qown.at[b], qc.at[b], s_q.at[b, 0], r_q.at[b, 0], twin).start()
        arrived(uu.at[b, :, pl.ds(W, W)], s_u.at[b], r_u.at[b])

    def scatter_over(b):
        def body(i, carry):
            zq = turn(z, i, NZ)
            hsend[b, zq] = part(b, yo, zq).astype(BF)
            far(hsend.at[b, zq, pl.ds(0, HALF)], hin.at[b, zq, pl.ds(0, HALF)],
                s_a.at[b, zq, 0], r_a.at[b, zq, 0], right).start()
            far(hsend.at[b, zq, pl.ds(HALF, HALF)], hin.at[b, zq, pl.ds(HALF, HALF)],
                s_a.at[b, zq, 1], r_a.at[b, zq, 1], left).start()
            return carry
        lax.fori_loop(1, NZ + 1, body, 0)

    def scatter_sides(b):
        arrived(qc.at[b], s_q.at[b, 0], r_q.at[b, 0])
        qsum[b, 0] = qown[b] + qc[b]
        for k in range(1, NY):
            far(qsum.at[b, 0], qy.at[b, k], s_q.at[b, k], r_q.at[b, k],
                at(z, turn(y, k, NY))).start()

        def body(i, carry):
            zq = turn(z, i, NZ)
            to_right = part(b, yr, zq)
            arrived(hin.at[b, zq, pl.ds(0, HALF)], s_a.at[b, zq, 0], r_a.at[b, zq, 0])
            fsend[b, zq, 0, :HALF] = (to_right[:HALF] + hin[b, zq, :HALF].astype(F32)).astype(BF)
            fsend[b, zq, 0, HALF:] = to_right[HALF:].astype(BF)
            far(fsend.at[b, zq, 0], fin.at[b, zq, 0], s_b.at[b, zq, 0], r_b.at[b, zq, 0], right).start()
            to_left = part(b, yl, zq)
            arrived(hin.at[b, zq, pl.ds(HALF, HALF)], s_a.at[b, zq, 1], r_a.at[b, zq, 1])
            fsend[b, zq, 1, :HALF] = to_left[:HALF].astype(BF)
            fsend[b, zq, 1, HALF:] = (to_left[HALF:] + hin[b, zq, HALF:].astype(F32)).astype(BF)
            far(fsend.at[b, zq, 1], fin.at[b, zq, 1], s_b.at[b, zq, 1], r_b.at[b, zq, 1], left).start()
            return carry
        lax.fori_loop(1, NZ + 1, body, 0)

    def own_column(b, zq):
        mine = part(b, y, zq)
        arrived(fin.at[b, zq, 0], s_b.at[b, zq, 0], r_b.at[b, zq, 0])
        arrived(fin.at[b, zq, 1], s_b.at[b, zq, 1], r_b.at[b, zq, 1])
        return mine + fin[b, zq, 0].astype(F32) + fin[b, zq, 1].astype(F32)

    def scatter_column(b):
        total = qsum[b, 0]
        for k in range(1, NY):
            arrived(qy.at[b, k], s_q.at[b, k], r_q.at[b, k])
            total = total + qy[b, k]
        qsum[b, 1] = total
        for k in range(1, NZ):
            far(qsum.at[b, 1], qz.at[b, k], s_q.at[b, 3 + k], r_q.at[b, 3 + k],
                at(turn(z, k, NZ), y)).start()

        def body(i, carry):
            zq = turn(z, i, NZ)
            zsend[b, zq] = own_column(b, zq).astype(BF)
            far(zsend.at[b, zq], zin.at[b, z], s_c.at[b, zq], r_c.at[b, z], at(zq, y)).start()
            return carry
        lax.fori_loop(1, NZ, body, 0)
        dnacc[...] = own_column(b, z)

    def gradient_end(b, g):
        total = qsum[b, 1]
        for k in range(1, NZ):
            arrived(qz.at[b, k], s_q.at[b, 3 + k], r_q.at[b, 3 + k])
            total = total + qz[b, k]
        row = jnp.sum(total, axis=0, keepdims=True)
        inner = jnp.broadcast_to(row, (128, TOK)).T[:, :1]
        dn = dnacc[...]
        for k in range(1, NZ):
            zq = turn(z, k, NZ)
            arrived(zin.at[b, zq], s_c.at[b, zq], r_c.at[b, zq])
            dn = dn + zin[b, zq].astype(F32)
        radius = rb[b][:, :1]
        mine = pl.multiple_of(tp * W, 128)
        x = xg[g, y, z].astype(F32)
        grad = (
            cot[b].astype(F32)
            + gv[:, pl.ds(mine, W)] * dn / radius
            - x * (inner / (width * radius * radius * radius))
        )
        outb[2 + b] = grad.astype(BF)

    def forward_end(g, slot):
        radius, h = hidden(g)
        outb[slot] = (xg[g, y, z].astype(F32) + gelu_value(h)).astype(BF)

    own_sends(B, fwd_in.at[0])
    far(stash_in.at[0, 0], xg.at[A, y, z], s_ev.at[0], r_ev.at[0], mirror).start()
    near(fwd_in.at[0], xg.at[B, y, z], l_in.at[0]).start()
    near(gain, gv, l_in.at[1]).start()
    near(cot_in.at[0], cot.at[0], l_in.at[2]).start()
    for k, yy in enumerate((y, yl, yr, yo)):
        near(weight.at[:, yy, core], wc.at[yy, :, :, pl.ds(0, W)], l_w.at[k]).start()
        far(weight.at[:, yy, 1 - core], wc.at[yy, :, :, pl.ds(W, W)], s_w.at[k], r_w.at[k], twin).start()
    far(stash_in.at[0, 1], xg.at[C, y, z], s_ev.at[1], r_ev.at[1], mirror).start()
    far(fwd_in.at[0], stash_out.at[0, 0], s_st.at[0], r_st.at[0], mirror).start()

    @pl.when(sec == 0)
    def _():
        near(fresh_in, xg.at[D, y, z], l_in.at[3]).start()

    @pl.when(sec == nsec - 1)
    def _():
        near(fresh_cot, cot.at[1], l_in.at[4]).start()

    acc[...] = jnp.zeros_like(acc)
    column_sends(B)
    near(fwd_in.at[0], xg.at[B, y, z], l_in.at[0]).wait()
    near(gain, gv, l_in.at[1]).wait()
    near(cot_in.at[0], cot.at[0], l_in.at[2]).wait()
    arrived(xg.at[A, y, z], s_ev.at[0], r_ev.at[0])
    own_sends(A, xg.at[A, y, z])
    for k, yy in enumerate((y, yl, yr, yo)):
        near(weight.at[:, yy, core], wc.at[yy, :, :, pl.ds(0, W)], l_w.at[k]).wait()
        arrived(wc.at[yy, :, :, pl.ds(W, W)], s_w.at[k], r_w.at[k])
    relay(B)
    column_sends(A)
    last_quarter(B)
    arrived(xg.at[C, y, z], s_ev.at[1], r_ev.at[1])
    own_sends(C, xg.at[C, y, z])
    forward_end(B, 0)

    @pl.when(sec < nsec - 1)
    def _():
        far(outb.at[0], xg.at[D, y, z], s_next, r_next, after).start()

    near(outb.at[0], first_out.at[0], l_out.at[0]).start()
    relay(A)
    column_sends(C)
    last_quarter(A)

    @pl.when(sec == 0)
    def _():
        near(fresh_in, xg.at[D, y, z], l_in.at[3]).wait()

    @pl.when(sec > 0)
    def _():
        arrived(xg.at[D, y, z], s_next, r_next)

    gradient_start(0, A)
    relay(C)
    scatter_over(0)
    last_quarter(C)
    scatter_sides(0)
    own_sends(D, xg.at[D, y, z])
    far(xg.at[D, y, z], stash_out.at[0, 1], s_st.at[1], r_st.at[1], mirror).start()
    column_sends(D)
    scatter_column(0)
    gradient_end(0, A)

    @pl.when(sec > 0)
    def _():
        far(outb.at[2], cot.at[1], s_prev, r_prev, before).start()

    near(outb.at[2], first_grad.at[0], l_out.at[2]).start()
    relay(D)

    @pl.when(sec == nsec - 1)
    def _():
        near(fresh_cot, cot.at[1], l_in.at[4]).wait()

    @pl.when(sec < nsec - 1)
    def _():
        arrived(cot.at[1], s_prev, r_prev)

    gradient_start(1, C)
    scatter_over(1)
    last_quarter(D)
    scatter_sides(1)
    forward_end(D, 1)
    near(outb.at[1], second_out.at[0], l_out.at[1]).start()
    scatter_column(1)
    gradient_end(1, C)
    near(outb.at[3], second_grad.at[0], l_out.at[3]).start()

    for g in range(4):
        own = fwd_in.at[0] if g == B else xg.at[g, y, z]
        for k in range(1, NZ):
            sent(own, s_z.at[g, k], r_z.at[g, z])

        def sends_of(i, carry):
            slot = xg.at[g, 0, i]
            half = slot.at[pl.ds(0, HALF)]
            for k in range(2):
                sent(slot, s_y.at[g, i, k], r_y.at[g, i, k])
                sent(half, s_r.at[g, i, k], r_r.at[g, i, k])
            return carry
        lax.fori_loop(0, NZ, sends_of, 0)
        sent(acc.at[g, :, pl.ds(W, W + 128)], s_h.at[g], r_h.at[g])
    for b in range(2):
        def sends_to(i, carry):
            for k in range(2):
                sent(hsend.at[b, i, pl.ds(0, HALF)], s_a.at[b, i, k], r_a.at[b, i, k])
                sent(fsend.at[b, i, k], s_b.at[b, i, k], r_b.at[b, i, k])
            return carry
        lax.fori_loop(0, NZ, sends_to, 0)

        def sends_up(i, carry):
            zq = turn(z, i, NZ)
            sent(zsend.at[b, zq], s_c.at[b, zq], r_c.at[b, zq])
            return carry
        lax.fori_loop(1, NZ, sends_up, 0)
        sent(uu.at[b, :, pl.ds(0, W)], s_u.at[b], r_u.at[b])
        for k in range(7):
            sent(qown.at[b], s_q.at[b, k], r_q.at[b, k])
        sent(stash_in.at[0, b], s_ev.at[b], r_ev.at[b])
        sent(fwd_in.at[0], s_st.at[b], r_st.at[b])
        arrived(stash_out.at[0, b], s_st.at[b], r_st.at[b])
    for k in range(4):
        sent(weight.at[:, 0, 0], s_w.at[k], r_w.at[k])
    @pl.when(sec < nsec - 1)
    def _():
        sent(outb.at[0], s_next, r_next)

    @pl.when(sec > 0)
    def _():
        sent(outb.at[2], s_prev, r_prev)

    for k, out in enumerate((first_out, second_out, first_grad, second_grad)):
        near(outb.at[k], out.at[0], l_out.at[k]).wait()


def shards(nsec, fresh_in, fwd_in, fresh_cot, cot_in, stash_in, weight, gain):
    weight = weight.reshape(NZ, NY, 2, W, W)
    block = jax.ShapeDtypeStruct((1, TOK, W), BF)
    dma = pltpu.SemaphoreType.DMA
    vm = pltpu.VMEM
    scratch = [
        vm((4, NY, NZ, TOK, W), BF),
        vm((NY, NZ, W, 2 * W), BF),
        vm((1, NY * NZ * 2 * W), F32),
        vm((4, TOK, 2 * W + 128), F32),
        vm((4, TOK, W + 128), F32),
        vm((2, TOK, 2 * W), BF),
        vm((2, TOK, W), BF),
        vm((4, TOK, W), BF),
        vm((2, TOK, 128), F32),
        vm((2, NZ, TOK, W), BF),
        vm((2, NZ, TOK, W), BF),
        vm((2, NZ, 2, TOK, W), BF),
        vm((2, NZ, 2, TOK, W), BF),
        vm((2, NZ, TOK, W), BF),
        vm((2, NZ, TOK, W), BF),
        vm((TOK, W), F32),
        vm((2, 8, 128), F32),
        vm((2, 8, 128), F32),
        vm((2, NY, 8, 128), F32),
        vm((2, NZ, 8, 128), F32),
        vm((2, 2, 8, 128), F32),
        dma((4, NZ)), dma((4, NZ)),
        dma((4, NZ, 2)), dma((4, NZ, 2)),
        dma((4, NZ, 2)), dma((4, NZ, 2)),
        dma((4,)), dma((4,)), dma((4,)),
        dma((4,)), dma((4,)), dma((2,)), dma((2,)),
        dma((2,)), dma((2,)), dma, dma, dma, dma, dma((2,)), dma((2,)),
        dma((5,)), dma((4,)),
        dma((2, NZ, 2)), dma((2, NZ, 2)), dma((2, NZ, 2)), dma((2, NZ, 2)),
        dma((2, NZ)), dma((2, NZ)),
        dma((2, 7)), dma((2, 7)),
    ]
    anywhere = pl.BlockSpec(memory_space=pl.ANY)
    return pl.pallas_call(
        functools.partial(kernel, nsec),
        out_shape=(block, block, block, block, jax.ShapeDtypeStruct((1, 2, TOK, W), BF)),
        in_specs=[anywhere] * 7,
        out_specs=(anywhere,) * 5,
        scratch_shapes=scratch,
        compiler_params=pltpu.CompilerParams(
            collective_id=0, has_side_effects=True, vmem_limit_bytes=56 * 2**20
        ),
        cost_estimate=pl.CostEstimate(flops=7_250_000_000, bytes_accessed=12_000_000, transcendentals=200_000),
    )(fresh_in, fwd_in, fresh_cot, cot_in, stash_in, weight, gain)


def solution(mesh):
    return jax.shard_map(
        functools.partial(shards, mesh.shape["section"]),
        mesh=mesh,
        in_specs=(
            P(None, "tp"),
            P("section", None, "tp"),
            P(None, "tp"),
            P("section", None, "tp"),
            P("section", None, None, "tp"),
            P("section", None, "tp"),
            P("section", None),
        ),
        out_specs=(
            P("section", None, "tp"),
            P("section", None, "tp"),
            P("section", None, "tp"),
            P("section", None, "tp"),
            P("section", None, None, "tp"),
        ),
        check_vma=False,
    )
```

```python
import functools

import jax
import jax.numpy as jnp
from jax import lax
from jax.experimental import pallas as pl
from jax.experimental.pallas import tpu as pltpu
from jax.sharding import PartitionSpec as P

EPS = 1e-05
GCOEF = 0.7978845608028654
MESH = pl.DeviceIdType.MESH

TOK = 128
W = 384
NZ = 4
NY = 4
HALF = TOK // 2
A, B, C, D = 0, 1, 2, 3
BF = jnp.bfloat16
F32 = jnp.float32


def gelu_value(h):
    return 0.5 * h * (1.0 + jnp.tanh(GCOEF * (h + 0.044715 * h * h * h)))


def gelu_slope(h):
    tval = jnp.tanh(GCOEF * (h + 0.044715 * h * h * h))
    return 0.5 * (1.0 + tval) + 0.5 * h * (1.0 - tval * tval) * GCOEF * (
        1.0 + 3.0 * 0.044715 * h * h
    )


def kernel(
    nsec,
    fresh_in, fwd_in, fresh_cot, cot_in, stash_in, weight, gain,
    first_out, second_out, first_grad, second_grad, stash_out,
    xg, wc, gv, acc, hr, uu, cot, outb, rb,
    hsend, hin, fsend, fin, zsend, zin, dnacc, qown, qc, qy, qz, qsum,
    s_z, r_z, s_y, r_y, s_r, r_r,
    s_w, r_w, l_w,
    s_h, r_h, s_u, r_u,
    s_ev, r_ev, s_next, r_next, s_prev, r_prev, s_st, r_st,
    l_in, l_out,
    s_a, r_a, s_b, r_b, s_c, r_c,
    s_q, r_q,
):
    sec = lax.axis_index("section")
    tp = lax.axis_index("tp")
    core = lax.rem(tp, 2)
    y = lax.rem(tp // 2, NY)
    z = tp // (2 * NY)
    width = NZ * NY * 2 * W

    def at(zz, yy, cc=None):
        return (sec, (zz * NY + yy) * 2 + (core if cc is None else cc))

    def turn(v, k, n):
        return lax.rem(v + k, n)

    yr, yl, yo = turn(y, 1, NY), turn(y, 3, NY), turn(y, 2, NY)
    right, left, over = at(z, yr), at(z, yl), at(z, yo)
    twin = at(z, y, 1 - core)
    mirror = (nsec - 1 - sec, tp)
    after = (turn(sec, 1, nsec), tp)
    before = (turn(sec, nsec - 1, nsec), tp)

    def far(src, dst, ssem, rsem, dev):
        return pltpu.make_async_remote_copy(
            src_ref=src, dst_ref=dst, send_sem=ssem, recv_sem=rsem,
            device_id=dev, device_id_type=MESH,
        )

    def arrived(dst, ssem, rsem):
        far(dst, dst, ssem, rsem, twin).wait_recv()

    def sent(src, ssem, rsem):
        far(src, src, ssem, rsem, twin).wait_send()

    def near(src, dst, sem):
        return pltpu.make_async_copy(src, dst, sem)

    for k, yy in enumerate((y, yl, yr, yo)):
        near(weight.at[:, yy, core], wc.at[yy, :, :, pl.ds(0, W)], l_w.at[k]).start()
    barrier = pltpu.get_barrier_semaphore()

    def greet(dev):
        pl.semaphore_signal(barrier, inc=1, device_id=dev, device_id_type=MESH)

    for k in range(1, NZ):
        greet(at(turn(z, k, NZ), y))
    for dev in (right, left, over, twin, mirror, after, before):
        greet(dev)
    pl.semaphore_wait(barrier, 10)

    below, above = at(turn(z, 3, NZ), y), at(turn(z, 1, NZ), y)

    def nearest(i):
        v = jnp.where((z == 0) | (z == 3), i, jnp.where(i < 2, 1 - i, i))
        return jnp.where(z < 2, v, 3 - v)

    def go_up(g, src, zq):
        far(src, xg.at[g, y, zq], s_z.at[g, zq, 0], r_z.at[g, zq], above).start()

    def go_down(g, src, zq):
        far(src, xg.at[g, y, zq], s_z.at[g, zq, 1], r_z.at[g, zq], below).start()

    def own_up(g, src):
        @pl.when(z < NZ - 1)
        def _():
            go_up(g, src, z)

        @pl.when(z > 0)
        def _():
            go_down(g, src, z)

    def own_across(g, src):
        far(src, xg.at[g, y, z], s_y.at[g, z, 0], r_y.at[g, z, 0], right).start()
        far(src, xg.at[g, y, z], s_y.at[g, z, 1], r_y.at[g, z, 1], left).start()

    def column_sends(g):
        def body(i, carry):
            zq = nearest(i)
            slot = xg.at[g, y, zq]
            arrived(slot, s_z.at[g, 0, 0], r_z.at[g, zq])

            @pl.when((zq < z) & (z < NZ - 1))
            def _():
                go_up(g, slot, zq)

            @pl.when((zq > z) & (z > 0))
            def _():
                go_down(g, slot, zq)

            far(slot, slot, s_y.at[g, zq, 0], r_y.at[g, zq, 0], right).start()
            far(slot, slot, s_y.at[g, zq, 1], r_y.at[g, zq, 1], left).start()
            return carry
        lax.fori_loop(1, NZ, body, 0)

    def product(g, yy, zq):
        x = xg[g, yy, zq].astype(F32)
        x2 = x * x
        acc[g, :, 2 * W:] += x2[:, :128] + x2[:, 128:256] + x2[:, 256:]
        start = pl.multiple_of(((zq * NY + yy) * 2 + core) * W, 128)
        n = (x * gv[:, pl.ds(start, W)]).astype(BF)
        acc[g, :, :2 * W] += jnp.dot(n, wc[yy, zq], preferred_element_type=F32)

    def relay(g):
        def body(i, carry):
            zq = nearest(i)
            from_left, from_right = xg.at[g, yl, zq], xg.at[g, yr, zq]
            arrived(from_left, s_z.at[g, 0, 0], r_y.at[g, zq, 0])
            top = from_left.at[pl.ds(0, HALF)]
            far(top, top, s_r.at[g, zq, 0], r_r.at[g, zq, 0], right).start()
            arrived(from_right, s_z.at[g, 0, 0], r_y.at[g, zq, 1])
            low = from_right.at[pl.ds(HALF, HALF)]
            far(low, low, s_r.at[g, zq, 1], r_r.at[g, zq, 1], left).start()
            product(g, y, zq)
            product(g, yl, zq)
            product(g, yr, zq)
            return carry
        lax.fori_loop(0, NZ, body, 0)

    def last_quarter(g):
        def body(i, carry):
            zq = nearest(i)
            slot = xg.at[g, yo, zq]
            arrived(slot.at[pl.ds(0, HALF)], s_z.at[g, 0, 0], r_r.at[g, zq, 0])
            arrived(slot.at[pl.ds(HALF, HALF)], s_z.at[g, 0, 0], r_r.at[g, zq, 1])
            product(g, yo, zq)
            return carry
        lax.fori_loop(0, NZ, body, 0)
        far(acc.at[g, :, pl.ds(W, W + 128)], hr.at[g], s_h.at[g], r_h.at[g], twin).start()

    def hidden(g):
        arrived(hr.at[g], s_z.at[g, 0, 0], r_h.at[g])
        ss = acc[g, :, 2 * W:] + hr[g, :, W:]
        radius = jnp.sqrt(jnp.sum(ss, axis=-1, keepdims=True) / width + EPS)
        h = (acc[g, :, :W] + hr[g, :, :W]) / radius
        return radius, h

    def part(b, yy, zq):
        return lax.dot_general(
            uu[b], wc[yy, zq], (((1,), (1,)), ((), ())), preferred_element_type=F32
        )

    def gradient_start(b, g):
        radius, h = hidden(g)
        u = (cot[b].astype(F32) * gelu_slope(h)).astype(BF)
        uu[b, :, :W] = u
        far(uu.at[b, :, pl.ds(0, W)], uu.at[b, :, pl.ds(W, W)], s_u.at[b], r_u.at[b], twin).start()
        rb[b] = jnp.broadcast_to(radius, (TOK, 128))
        e = u.astype(F32) * h
        lanes = (e[:, :128] + e[:, 128:256] + e[:, 256:]) * radius
        t = lanes.T
        q = t[0:8]
        for k in range(1, 16):
            q = q + t[8 * k:8 * k + 8]
        qown[b] = q
        far(qown.at[b], qc.at[b], s_q.at[b, 0], r_q.at[b, 0], twin).start()
        arrived(uu.at[b, :, pl.ds(W, W)], s_u.at[b], r_u.at[b])

    def scatter_over(b):
        def body(i, carry):
            zq = turn(z, i, NZ)
            hsend[b, zq] = part(b, yo, zq).astype(BF)
            far(hsend.at[b, zq, pl.ds(0, HALF)], hin.at[b, zq, pl.ds(0, HALF)],
                s_a.at[b, zq, 0], r_a.at[b, zq, 0], right).start()
            far(hsend.at[b, zq, pl.ds(HALF, HALF)], hin.at[b, zq, pl.ds(HALF, HALF)],
                s_a.at[b, zq, 1], r_a.at[b, zq, 1], left).start()
            return carry
        lax.fori_loop(1, NZ + 1, body, 0)

    def scatter_sides(b):
        arrived(qc.at[b], s_q.at[b, 0], r_q.at[b, 0])
        qsum[b, 0] = qown[b] + qc[b]
        for k in range(1, NY):
            far(qsum.at[b, 0], qy.at[b, k], s_q.at[b, k], r_q.at[b, k],
                at(z, turn(y, k, NY))).start()

        def body(i, carry):
            zq = turn(z, i, NZ)
            to_right = part(b, yr, zq)
            arrived(hin.at[b, zq, pl.ds(0, HALF)], s_a.at[b, zq, 0], r_a.at[b, zq, 0])
            fsend[b, zq, 0, :HALF] = (to_right[:HALF] + hin[b, zq, :HALF].astype(F32)).astype(BF)
            fsend[b, zq, 0, HALF:] = to_right[HALF:].astype(BF)
            far(fsend.at[b, zq, 0], fin.at[b, zq, 0], s_b.at[b, zq, 0], r_b.at[b, zq, 0], right).start()
            to_left = part(b, yl, zq)
            arrived(hin.at[b, zq, pl.ds(HALF, HALF)], s_a.at[b, zq, 1], r_a.at[b, zq, 1])
            fsend[b, zq, 1, :HALF] = to_left[:HALF].astype(BF)
            fsend[b, zq, 1, HALF:] = (to_left[HALF:] + hin[b, zq, HALF:].astype(F32)).astype(BF)
            far(fsend.at[b, zq, 1], fin.at[b, zq, 1], s_b.at[b, zq, 1], r_b.at[b, zq, 1], left).start()
            return carry
        lax.fori_loop(1, NZ + 1, body, 0)

    def own_column(b, zq):
        mine = part(b, y, zq)
        arrived(fin.at[b, zq, 0], s_b.at[b, zq, 0], r_b.at[b, zq, 0])
        arrived(fin.at[b, zq, 1], s_b.at[b, zq, 1], r_b.at[b, zq, 1])
        return mine + fin[b, zq, 0].astype(F32) + fin[b, zq, 1].astype(F32)

    def scatter_column(b):
        total = qsum[b, 0]
        for k in range(1, NY):
            arrived(qy.at[b, k], s_q.at[b, k], r_q.at[b, k])
            total = total + qy[b, k]
        qsum[b, 1] = total
        for k in range(1, NZ):
            far(qsum.at[b, 1], qz.at[b, k], s_q.at[b, 3 + k], r_q.at[b, 3 + k],
                at(turn(z, k, NZ), y)).start()

        def body(i, carry):
            zq = turn(z, i, NZ)
            zsend[b, zq] = own_column(b, zq).astype(BF)
            far(zsend.at[b, zq], zin.at[b, z], s_c.at[b, zq], r_c.at[b, z], at(zq, y)).start()
            return carry
        lax.fori_loop(1, NZ, body, 0)
        dnacc[...] = own_column(b, z)

    def gradient_end(b, g):
        total = qsum[b, 1]
        for k in range(1, NZ):
            arrived(qz.at[b, k], s_q.at[b, 3 + k], r_q.at[b, 3 + k])
            total = total + qz[b, k]
        row = jnp.sum(total, axis=0, keepdims=True)
        inner = jnp.broadcast_to(row, (128, TOK)).T[:, :1]
        dn = dnacc[...]
        for k in range(1, NZ):
            zq = turn(z, k, NZ)
            arrived(zin.at[b, zq], s_c.at[b, zq], r_c.at[b, zq])
            dn = dn + zin[b, zq].astype(F32)
        radius = rb[b][:, :1]
        mine = pl.multiple_of(tp * W, 128)
        x = xg[g, y, z].astype(F32)
        grad = (
            cot[b].astype(F32)
            + gv[:, pl.ds(mine, W)] * dn / radius
            - x * (inner / (width * radius * radius * radius))
        )
        outb[2 + b] = grad.astype(BF)

    def forward_end(g, slot):
        radius, h = hidden(g)
        outb[slot] = (xg[g, y, z].astype(F32) + gelu_value(h)).astype(BF)

    def mine(g):
        return xg.at[g, y, z]

    def weight_in():
        for k, yy in enumerate((y, yl, yr, yo)):
            far(weight.at[:, yy, 1 - core], wc.at[yy, :, :, pl.ds(W, W)], s_w.at[k], r_w.at[k], twin).start()

    def small_in():
        near(fwd_in.at[0], mine(B), l_in.at[0]).start()
        near(gain, gv, l_in.at[1]).start()
        near(cot_in.at[0], cot.at[0], l_in.at[2]).start()

        @pl.when(sec == 0)
        def _():
            near(fresh_in, mine(D), l_in.at[3]).start()

        @pl.when(sec == nsec - 1)
        def _():
            near(fresh_cot, cot.at[1], l_in.at[4]).start()

        acc[...] = jnp.zeros_like(acc)

    def small_wait():
        near(fwd_in.at[0], mine(B), l_in.at[0]).wait()
        near(gain, gv, l_in.at[1]).wait()
        near(cot_in.at[0], cot.at[0], l_in.at[2]).wait()

    def weight_wait():
        for k, yy in enumerate((y, yl, yr, yo)):
            near(weight.at[:, yy, core], wc.at[yy, :, :, pl.ds(0, W)], l_w.at[k]).wait()
            arrived(wc.at[yy, :, :, pl.ds(W, W)], s_w.at[k], r_w.at[k])

    def saved_in(b, g):
        far(stash_in.at[0, b], mine(g), s_ev.at[b], r_ev.at[b], mirror).start()

    def saved_wait(b, g):
        arrived(mine(g), s_ev.at[b], r_ev.at[b])

    def stash_first():
        far(mine(B), stash_out.at[0, 0], s_st.at[0], r_st.at[0], mirror).start()

    def stash_second():
        far(mine(D), stash_out.at[0, 1], s_st.at[1], r_st.at[1], mirror).start()

    def next_in():
        @pl.when(sec < nsec - 1)
        def _():
            far(outb.at[0], mine(D), s_next, r_next, after).start()

        near(outb.at[0], first_out.at[0], l_out.at[0]).start()

    def next_wait():
        @pl.when(sec == 0)
        def _():
            near(fresh_in, mine(D), l_in.at[3]).wait()

        @pl.when(sec > 0)
        def _():
            arrived(mine(D), s_next, r_next)

    def cot_out():
        @pl.when(sec > 0)
        def _():
            far(outb.at[2], cot.at[1], s_prev, r_prev, before).start()

        near(outb.at[2], first_grad.at[0], l_out.at[2]).start()

    def cot_wait():
        @pl.when(sec == nsec - 1)
        def _():
            near(fresh_cot, cot.at[1], l_in.at[4]).wait()

        @pl.when(sec < nsec - 1)
        def _():
            arrived(cot.at[1], s_prev, r_prev)

    def second_done():
        near(outb.at[1], second_out.at[0], l_out.at[1]).start()

    def grad_done():
        near(outb.at[3], second_grad.at[0], l_out.at[3]).start()

    saved_in(0, A)
    own_up(B, fwd_in.at[0])
    own_across(B, fwd_in.at[0])
    weight_in()
    small_in()
    column_sends(B)
    small_wait()
    saved_wait(0, A)
    own_up(A, mine(A))
    own_across(A, mine(A))
    saved_in(1, C)
    weight_wait()
    relay(B)
    column_sends(A)
    last_quarter(B)
    forward_end(B, 0)
    next_in()
    relay(A)
    saved_wait(1, C)
    own_up(C, mine(C))
    last_quarter(A)
    own_across(C, mine(C))
    next_wait()
    own_up(D, mine(D))
    gradient_start(0, A)
    scatter_over(0)
    scatter_sides(0)
    column_sends(C)
    stash_first()
    scatter_column(0)
    relay(C)
    gradient_end(0, A)
    cot_out()
    last_quarter(C)
    own_across(D, mine(D))
    column_sends(D)
    stash_second()
    cot_wait()
    gradient_start(1, C)
    scatter_over(1)
    relay(D)
    scatter_sides(1)
    last_quarter(D)
    scatter_column(1)
    forward_end(D, 1)
    second_done()
    gradient_end(1, C)
    grad_done()

    for g in range(4):
        def sends_of(i, carry):
            slot = xg.at[g, 0, i]

            @pl.when((i <= z) & (z < NZ - 1))
            def _():
                sent(slot, s_z.at[g, i, 0], r_z.at[g, i])

            @pl.when((i >= z) & (z > 0))
            def _():
                sent(slot, s_z.at[g, i, 1], r_z.at[g, i])

            half = slot.at[pl.ds(0, HALF)]
            for k in range(2):
                sent(slot, s_y.at[g, i, k], r_y.at[g, i, k])
                sent(half, s_r.at[g, i, k], r_r.at[g, i, k])
            return carry
        lax.fori_loop(0, NZ, sends_of, 0)
        sent(acc.at[g, :, pl.ds(W, W + 128)], s_h.at[g], r_h.at[g])
    for b in range(2):
        def sends_to(i, carry):
            for k in range(2):
                sent(hsend.at[b, i, pl.ds(0, HALF)], s_a.at[b, i, k], r_a.at[b, i, k])
                sent(fsend.at[b, i, k], s_b.at[b, i, k], r_b.at[b, i, k])
            return carry
        lax.fori_loop(0, NZ, sends_to, 0)

        def sends_up(i, carry):
            zq = turn(z, i, NZ)
            sent(zsend.at[b, zq], s_c.at[b, zq], r_c.at[b, zq])
            return carry
        lax.fori_loop(1, NZ, sends_up, 0)
        sent(uu.at[b, :, pl.ds(0, W)], s_u.at[b], r_u.at[b])
        for k in range(7):
            sent(qown.at[b], s_q.at[b, k], r_q.at[b, k])
        sent(stash_in.at[0, b], s_ev.at[b], r_ev.at[b])
        sent(fwd_in.at[0], s_st.at[b], r_st.at[b])
        arrived(stash_out.at[0, b], s_st.at[b], r_st.at[b])
    for k in range(4):
        sent(weight.at[:, 0, 0], s_w.at[k], r_w.at[k])
    @pl.when(sec < nsec - 1)
    def _():
        sent(outb.at[0], s_next, r_next)

    @pl.when(sec > 0)
    def _():
        sent(outb.at[2], s_prev, r_prev)

    for k, out in enumerate((first_out, second_out, first_grad, second_grad)):
        near(outb.at[k], out.at[0], l_out.at[k]).wait()


def hand_over(*refs):
    for k in range(5):
        refs[5 + k][...] = refs[k][...]


def shards(nsec, fresh_in, fwd_in, fresh_cot, cot_in, stash_in, weight, gain):
    weight = weight.reshape(NZ, NY, 2, W, W)
    block = jax.ShapeDtypeStruct((1, TOK, W), BF)
    dma = pltpu.SemaphoreType.DMA
    vm = pltpu.VMEM
    scratch = [
        vm((4, NY, NZ, TOK, W), BF),
        vm((NY, NZ, W, 2 * W), BF),
        vm((1, NY * NZ * 2 * W), F32),
        vm((4, TOK, 2 * W + 128), F32),
        vm((4, TOK, W + 128), F32),
        vm((2, TOK, 2 * W), BF),
        vm((2, TOK, W), BF),
        vm((4, TOK, W), BF),
        vm((2, TOK, 128), F32),
        vm((2, NZ, TOK, W), BF),
        vm((2, NZ, TOK, W), BF),
        vm((2, NZ, 2, TOK, W), BF),
        vm((2, NZ, 2, TOK, W), BF),
        vm((2, NZ, TOK, W), BF),
        vm((2, NZ, TOK, W), BF),
        vm((TOK, W), F32),
        vm((2, 8, 128), F32),
        vm((2, 8, 128), F32),
        vm((2, NY, 8, 128), F32),
        vm((2, NZ, 8, 128), F32),
        vm((2, 2, 8, 128), F32),
        dma((4, NZ, 2)), dma((4, NZ)),
        dma((4, NZ, 2)), dma((4, NZ, 2)),
        dma((4, NZ, 2)), dma((4, NZ, 2)),
        dma((4,)), dma((4,)), dma((4,)),
        dma((4,)), dma((4,)), dma((2,)), dma((2,)),
        dma((2,)), dma((2,)), dma, dma, dma, dma, dma((2,)), dma((2,)),
        dma((5,)), dma((4,)),
        dma((2, NZ, 2)), dma((2, NZ, 2)), dma((2, NZ, 2)), dma((2, NZ, 2)),
        dma((2, NZ)), dma((2, NZ)),
        dma((2, 7)), dma((2, 7)),
    ]
    anywhere = pl.BlockSpec(memory_space=pl.ANY)
    outs = pl.pallas_call(
        functools.partial(kernel, nsec),
        out_shape=(block, block, block, block, jax.ShapeDtypeStruct((1, 2, TOK, W), BF)),
        in_specs=[anywhere] * 7,
        out_specs=(anywhere,) * 5,
        scratch_shapes=scratch,
        compiler_params=pltpu.CompilerParams(
            collective_id=0, has_side_effects=True, vmem_limit_bytes=56 * 2**20
        ),
        cost_estimate=pl.CostEstimate(flops=7_250_000_000, bytes_accessed=12_000_000, transcendentals=200_000),
    )(fresh_in, fwd_in, fresh_cot, cot_in, stash_in, weight, gain)
    return pl.pallas_call(
        hand_over,
        out_shape=tuple(jax.ShapeDtypeStruct(o.shape, o.dtype) for o in outs),
    )(*outs)


def solution(mesh):
    return jax.shard_map(
        functools.partial(shards, mesh.shape["section"]),
        mesh=mesh,
        in_specs=(
            P(None, "tp"),
            P("section", None, "tp"),
            P(None, "tp"),
            P("section", None, "tp"),
            P("section", None, None, "tp"),
            P("section", None, "tp"),
            P("section", None),
        ),
        out_specs=(
            P("section", None, "tp"),
            P("section", None, "tp"),
            P("section", None, "tp"),
            P("section", None, "tp"),
            P("section", None, None, "tp"),
        ),
        check_vma=False,
    )
```

```python
import functools

import jax
import jax.numpy as jnp
from jax import lax
from jax.experimental import pallas as pl
from jax.experimental.pallas import tpu as pltpu
from jax.sharding import PartitionSpec as P

EPS = 1e-05
GCOEF = 0.7978845608028654
MESH = pl.DeviceIdType.MESH

TOK = 128
W = 384
NZ = 4
NY = 4
HALF = TOK // 2
A, B, C, D = 0, 1, 2, 3
UNI = (A, C, D,)
BF = jnp.bfloat16
F32 = jnp.float32


def gelu_value(h):
    return 0.5 * h * (1.0 + jnp.tanh(GCOEF * (h + 0.044715 * h * h * h)))


def gelu_slope(h):
    tval = jnp.tanh(GCOEF * (h + 0.044715 * h * h * h))
    return 0.5 * (1.0 + tval) + 0.5 * h * (1.0 - tval * tval) * GCOEF * (
        1.0 + 3.0 * 0.044715 * h * h
    )


def kernel(
    nsec,
    fresh_in, fwd_in, fresh_cot, cot_in, stash_in, weight, gain,
    first_out, second_out, first_grad, second_grad, stash_out,
    xg, wc, gv, acc, hr, uu, cot, outb, rb,
    hsend, hin, fsend, fin, zsend, zin, dnacc, qown, qc, qy, qz, qsum,
    s_z, r_z, s_y, r_y, s_r, r_r,
    s_w, r_w, l_w,
    s_h, r_h, s_u, r_u,
    s_ev, r_ev, s_next, r_next, s_prev, r_prev, s_st, r_st,
    l_in, l_out,
    s_a, r_a, s_b, r_b, s_c, r_c,
    s_q, r_q,
):
    sec = lax.axis_index("section")
    tp = lax.axis_index("tp")
    core = lax.rem(tp, 2)
    y = lax.rem(tp // 2, NY)
    z = tp // (2 * NY)
    width = NZ * NY * 2 * W

    def at(zz, yy, cc=None):
        return (sec, (zz * NY + yy) * 2 + (core if cc is None else cc))

    def turn(v, k, n):
        return lax.rem(v + k, n)

    yr, yl, yo = turn(y, 1, NY), turn(y, 3, NY), turn(y, 2, NY)
    right, left, over = at(z, yr), at(z, yl), at(z, yo)
    twin = at(z, y, 1 - core)
    mirror = (nsec - 1 - sec, tp)
    after = (turn(sec, 1, nsec), tp)
    before = (turn(sec, nsec - 1, nsec), tp)

    def far(src, dst, ssem, rsem, dev):
        return pltpu.make_async_remote_copy(
            src_ref=src, dst_ref=dst, send_sem=ssem, recv_sem=rsem,
            device_id=dev, device_id_type=MESH,
        )

    def arrived(dst, ssem, rsem):
        far(dst, dst, ssem, rsem, twin).wait_recv()

    def sent(src, ssem, rsem):
        far(src, src, ssem, rsem, twin).wait_send()

    def near(src, dst, sem):
        return pltpu.make_async_copy(src, dst, sem)

    def local_in():
        near(fwd_in.at[0], xg.at[B, y, z], l_in.at[0]).start()
        near(gain, gv, l_in.at[1]).start()
        near(cot_in.at[0], cot.at[0], l_in.at[2]).start()

        @pl.when(sec == 0)
        def _():
            near(fresh_in, xg.at[D, y, z], l_in.at[3]).start()

        @pl.when(sec == nsec - 1)
        def _():
            near(fresh_cot, cot.at[1], l_in.at[4]).start()

        acc[...] = jnp.zeros_like(acc)

    for k, yy in enumerate((y, yl, yr, yo)):
        near(weight.at[:, yy, core], wc.at[yy, :, :, pl.ds(0, W)], l_w.at[k]).start()
    barrier = pltpu.get_barrier_semaphore()

    def greet(dev):
        pl.semaphore_signal(barrier, inc=1, device_id=dev, device_id_type=MESH)

    for k in range(1, NZ):
        greet(at(turn(z, k, NZ), y))
    for dev in (right, left, over, twin, mirror, after, before):
        greet(dev)
    local_in()
    pl.semaphore_wait(barrier, 10)

    below, above = at(turn(z, 3, NZ), y), at(turn(z, 1, NZ), y)

    def nearest(i):
        v = jnp.where((z == 0) | (z == 3), i, jnp.where(i < 2, 1 - i, i))
        return jnp.where(z < 2, v, 3 - v)

    def go_up(g, src, zq):
        far(src, xg.at[g, y, zq], s_z.at[g, zq, 0], r_z.at[g, zq], above).start()

    def go_down(g, src, zq):
        far(src, xg.at[g, y, zq], s_z.at[g, zq, 1], r_z.at[g, zq], below).start()

    def own_up(g, src):
        if g in UNI:
            for k in range(1, NZ):
                far(src, xg.at[g, y, z], s_z.at[g, k, 0], r_z.at[g, z],
                    at(turn(z, k, NZ), y)).start()
            return

        @pl.when(z < NZ - 1)
        def _():
            go_up(g, src, z)

        @pl.when(z > 0)
        def _():
            go_down(g, src, z)

    def own_across(g, src):
        far(src, xg.at[g, y, z], s_y.at[g, z, 0], r_y.at[g, z, 0], right).start()
        far(src, xg.at[g, y, z], s_y.at[g, z, 1], r_y.at[g, z, 1], left).start()

    def column_sends(g):
        def body(i, carry):
            zq = nearest(i)
            slot = xg.at[g, y, zq]
            arrived(slot, s_z.at[g, 0, 0], r_z.at[g, zq])

            if g not in UNI:
                @pl.when((zq < z) & (z < NZ - 1))
                def _():
                    go_up(g, slot, zq)

                @pl.when((zq > z) & (z > 0))
                def _():
                    go_down(g, slot, zq)

            far(slot, slot, s_y.at[g, zq, 0], r_y.at[g, zq, 0], right).start()
            far(slot, slot, s_y.at[g, zq, 1], r_y.at[g, zq, 1], left).start()
            return carry
        lax.fori_loop(1, NZ, body, 0)

    def product(g, yy, zq):
        x = xg[g, yy, zq].astype(F32)
        x2 = x * x
        acc[g, :, 2 * W:] += x2[:, :128] + x2[:, 128:256] + x2[:, 256:]
        start = pl.multiple_of(((zq * NY + yy) * 2 + core) * W, 128)
        n = (x * gv[:, pl.ds(start, W)]).astype(BF)
        acc[g, :, :2 * W] += jnp.dot(n, wc[yy, zq], preferred_element_type=F32)

    def relay(g):
        def body(i, carry):
            zq = nearest(i)
            from_left, from_right = xg.at[g, yl, zq], xg.at[g, yr, zq]
            arrived(from_left, s_z.at[g, 0, 0], r_y.at[g, zq, 0])
            top = from_left.at[pl.ds(0, HALF)]
            far(top, top, s_r.at[g, zq, 0], r_r.at[g, zq, 0], right).start()
            arrived(from_right, s_z.at[g, 0, 0], r_y.at[g, zq, 1])
            low = from_right.at[pl.ds(HALF, HALF)]
            far(low, low, s_r.at[g, zq, 1], r_r.at[g, zq, 1], left).start()
            product(g, y, zq)
            product(g, yl, zq)
            product(g, yr, zq)
            return carry
        lax.fori_loop(0, NZ, body, 0)

    def last_quarter(g):
        def body(i, carry):
            zq = nearest(i)
            slot = xg.at[g, yo, zq]
            arrived(slot.at[pl.ds(0, HALF)], s_z.at[g, 0, 0], r_r.at[g, zq, 0])
            arrived(slot.at[pl.ds(HALF, HALF)], s_z.at[g, 0, 0], r_r.at[g, zq, 1])
            product(g, yo, zq)
            return carry
        lax.fori_loop(0, NZ, body, 0)
        far(acc.at[g, :, pl.ds(W, W + 128)], hr.at[g], s_h.at[g], r_h.at[g], twin).start()

    def hidden(g):
        arrived(hr.at[g], s_z.at[g, 0, 0], r_h.at[g])
        ss = acc[g, :, 2 * W:] + hr[g, :, W:]
        radius = jnp.sqrt(jnp.sum(ss, axis=-1, keepdims=True) / width + EPS)
        h = (acc[g, :, :W] + hr[g, :, :W]) / radius
        return radius, h

    def part(b, yy, zq):
        return lax.dot_general(
            uu[b], wc[yy, zq], (((1,), (1,)), ((), ())), preferred_element_type=F32
        )

    def gradient_start(b, g):
        radius, h = hidden(g)
        u = (cot[b].astype(F32) * gelu_slope(h)).astype(BF)
        uu[b, :, :W] = u
        far(uu.at[b, :, pl.ds(0, W)], uu.at[b, :, pl.ds(W, W)], s_u.at[b], r_u.at[b], twin).start()
        rb[b] = jnp.broadcast_to(radius, (TOK, 128))
        e = u.astype(F32) * h
        lanes = (e[:, :128] + e[:, 128:256] + e[:, 256:]) * radius
        t = lanes.T
        q = t[0:8]
        for k in range(1, 16):
            q = q + t[8 * k:8 * k + 8]
        qown[b] = q
        far(qown.at[b], qc.at[b], s_q.at[b, 0], r_q.at[b, 0], twin).start()
        arrived(uu.at[b, :, pl.ds(W, W)], s_u.at[b], r_u.at[b])

    def scatter_over(b):
        def body(i, carry):
            zq = nearest(NZ - i)
            hsend[b, zq] = part(b, yo, zq).astype(BF)
            far(hsend.at[b, zq, pl.ds(0, HALF)], hin.at[b, zq, pl.ds(0, HALF)],
                s_a.at[b, zq, 0], r_a.at[b, zq, 0], right).start()
            far(hsend.at[b, zq, pl.ds(HALF, HALF)], hin.at[b, zq, pl.ds(HALF, HALF)],
                s_a.at[b, zq, 1], r_a.at[b, zq, 1], left).start()
            return carry
        lax.fori_loop(1, NZ + 1, body, 0)

    def scatter_sides(b):
        arrived(qc.at[b], s_q.at[b, 0], r_q.at[b, 0])
        qsum[b, 0] = qown[b] + qc[b]
        for k in range(1, NY):
            far(qsum.at[b, 0], qy.at[b, k], s_q.at[b, k], r_q.at[b, k],
                at(z, turn(y, k, NY))).start()

        def body(i, carry):
            zq = nearest(NZ - i)
            to_right = part(b, yr, zq)
            arrived(hin.at[b, zq, pl.ds(0, HALF)], s_a.at[b, zq, 0], r_a.at[b, zq, 0])
            fsend[b, zq, 0, :HALF] = (to_right[:HALF] + hin[b, zq, :HALF].astype(F32)).astype(BF)
            fsend[b, zq, 0, HALF:] = to_right[HALF:].astype(BF)
            far(fsend.at[b, zq, 0], fin.at[b, zq, 0], s_b.at[b, zq, 0], r_b.at[b, zq, 0], right).start()
            to_left = part(b, yl, zq)
            arrived(hin.at[b, zq, pl.ds(HALF, HALF)], s_a.at[b, zq, 1], r_a.at[b, zq, 1])
            fsend[b, zq, 1, :HALF] = to_left[:HALF].astype(BF)
            fsend[b, zq, 1, HALF:] = (to_left[HALF:] + hin[b, zq, HALF:].astype(F32)).astype(BF)
            far(fsend.at[b, zq, 1], fin.at[b, zq, 1], s_b.at[b, zq, 1], r_b.at[b, zq, 1], left).start()
            return carry
        lax.fori_loop(1, NZ + 1, body, 0)

    def own_column(b, zq):
        mine = part(b, y, zq)
        arrived(fin.at[b, zq, 0], s_b.at[b, zq, 0], r_b.at[b, zq, 0])
        arrived(fin.at[b, zq, 1], s_b.at[b, zq, 1], r_b.at[b, zq, 1])
        return mine + fin[b, zq, 0].astype(F32) + fin[b, zq, 1].astype(F32)

    def scatter_column(b):
        total = qsum[b, 0]
        for k in range(1, NY):
            arrived(qy.at[b, k], s_q.at[b, k], r_q.at[b, k])
            total = total + qy[b, k]
        qsum[b, 1] = total
        for k in range(1, NZ):
            far(qsum.at[b, 1], qz.at[b, k], s_q.at[b, 3 + k], r_q.at[b, 3 + k],
                at(turn(z, k, NZ), y)).start()

        def body(i, carry):
            zq = nearest(NZ - i)
            zsend[b, zq] = own_column(b, zq).astype(BF)
            far(zsend.at[b, zq], zin.at[b, z], s_c.at[b, zq], r_c.at[b, z], at(zq, y)).start()
            return carry
        lax.fori_loop(1, NZ, body, 0)
        dnacc[...] = own_column(b, z)

    def gradient_end(b, g):
        total = qsum[b, 1]
        for k in range(1, NZ):
            arrived(qz.at[b, k], s_q.at[b, 3 + k], r_q.at[b, 3 + k])
            total = total + qz[b, k]
        row = jnp.sum(total, axis=0, keepdims=True)
        inner = jnp.broadcast_to(row, (128, TOK)).T[:, :1]
        dn = dnacc[...]
        for k in range(1, NZ):
            zq = turn(z, k, NZ)
            arrived(zin.at[b, zq], s_c.at[b, zq], r_c.at[b, zq])
            dn = dn + zin[b, zq].astype(F32)
        radius = rb[b][:, :1]
        mine = pl.multiple_of(tp * W, 128)
        x = xg[g, y, z].astype(F32)
        grad = (
            cot[b].astype(F32)
            + gv[:, pl.ds(mine, W)] * dn / radius
            - x * (inner / (width * radius * radius * radius))
        )
        outb[2 + b] = grad.astype(BF)

    def forward_end(g, slot):
        radius, h = hidden(g)
        outb[slot] = (xg[g, y, z].astype(F32) + gelu_value(h)).astype(BF)

    def mine(g):
        return xg.at[g, y, z]

    def weight_in():
        for k, yy in enumerate((y, yl, yr, yo)):
            far(weight.at[:, yy, 1 - core], wc.at[yy, :, :, pl.ds(W, W)], s_w.at[k], r_w.at[k], twin).start()

    def small_wait():
        near(fwd_in.at[0], mine(B), l_in.at[0]).wait()
        near(gain, gv, l_in.at[1]).wait()
        near(cot_in.at[0], cot.at[0], l_in.at[2]).wait()

    def weight_wait():
        for k, yy in enumerate((y, yl, yr, yo)):
            near(weight.at[:, yy, core], wc.at[yy, :, :, pl.ds(0, W)], l_w.at[k]).wait()
            arrived(wc.at[yy, :, :, pl.ds(W, W)], s_w.at[k], r_w.at[k])

    def saved_in(b, g):
        far(stash_in.at[0, b], mine(g), s_ev.at[b], r_ev.at[b], mirror).start()

    def saved_wait(b, g):
        arrived(mine(g), s_ev.at[b], r_ev.at[b])

    def stash_first():
        far(mine(B), stash_out.at[0, 0], s_st.at[0], r_st.at[0], mirror).start()

    def stash_second():
        far(mine(D), stash_out.at[0, 1], s_st.at[1], r_st.at[1], mirror).start()

    def next_in():
        @pl.when(sec < nsec - 1)
        def _():
            far(outb.at[0], mine(D), s_next, r_next, after).start()

        near(outb.at[0], first_out.at[0], l_out.at[0]).start()

    def next_wait():
        @pl.when(sec == 0)
        def _():
            near(fresh_in, mine(D), l_in.at[3]).wait()

        @pl.when(sec > 0)
        def _():
            arrived(mine(D), s_next, r_next)

    def cot_out():
        @pl.when(sec > 0)
        def _():
            far(outb.at[2], cot.at[1], s_prev, r_prev, before).start()

        near(outb.at[2], first_grad.at[0], l_out.at[2]).start()

    def cot_wait():
        @pl.when(sec == nsec - 1)
        def _():
            near(fresh_cot, cot.at[1], l_in.at[4]).wait()

        @pl.when(sec < nsec - 1)
        def _():
            arrived(cot.at[1], s_prev, r_prev)

    def second_done():
        near(outb.at[1], second_out.at[0], l_out.at[1]).start()

    def grad_done():
        near(outb.at[3], second_grad.at[0], l_out.at[3]).start()

    saved_in(0, A)
    own_up(B, fwd_in.at[0])
    own_across(B, fwd_in.at[0])
    weight_in()
    column_sends(B)
    small_wait()
    saved_wait(0, A)
    own_up(A, mine(A))
    own_across(A, mine(A))
    saved_in(1, C)
    weight_wait()
    relay(B)
    column_sends(A)
    last_quarter(B)
    forward_end(B, 0)
    next_in()
    relay(A)
    saved_wait(1, C)
    own_up(C, mine(C))
    last_quarter(A)
    own_across(C, mine(C))
    next_wait()
    own_up(D, mine(D))
    gradient_start(0, A)
    scatter_over(0)
    scatter_sides(0)
    column_sends(C)
    stash_first()
    scatter_column(0)
    relay(C)
    own_across(D, mine(D))
    column_sends(D)
    gradient_end(0, A)
    cot_out()
    last_quarter(C)
    stash_second()
    cot_wait()
    gradient_start(1, C)
    scatter_over(1)
    relay(D)
    scatter_sides(1)
    last_quarter(D)
    scatter_column(1)
    forward_end(D, 1)
    second_done()
    gradient_end(1, C)
    grad_done()

    for g in range(4):
        if g in UNI:
            for k in range(1, NZ):
                sent(xg.at[g, y, z], s_z.at[g, k, 0], r_z.at[g, z])

        def sends_of(i, carry):
            slot = xg.at[g, 0, i]

            if g not in UNI:
                @pl.when((i <= z) & (z < NZ - 1))
                def _():
                    sent(slot, s_z.at[g, i, 0], r_z.at[g, i])

                @pl.when((i >= z) & (z > 0))
                def _():
                    sent(slot, s_z.at[g, i, 1], r_z.at[g, i])

            half = slot.at[pl.ds(0, HALF)]
            for k in range(2):
                sent(slot, s_y.at[g, i, k], r_y.at[g, i, k])
                sent(half, s_r.at[g, i, k], r_r.at[g, i, k])
            return carry
        lax.fori_loop(0, NZ, sends_of, 0)
        sent(acc.at[g, :, pl.ds(W, W + 128)], s_h.at[g], r_h.at[g])
    for b in range(2):
        def sends_to(i, carry):
            for k in range(2):
                sent(hsend.at[b, i, pl.ds(0, HALF)], s_a.at[b, i, k], r_a.at[b, i, k])
                sent(fsend.at[b, i, k], s_b.at[b, i, k], r_b.at[b, i, k])
            return carry
        lax.fori_loop(0, NZ, sends_to, 0)

        def sends_up(i, carry):
            zq = turn(z, i, NZ)
            sent(zsend.at[b, zq], s_c.at[b, zq], r_c.at[b, zq])
            return carry
        lax.fori_loop(1, NZ, sends_up, 0)
        sent(uu.at[b, :, pl.ds(0, W)], s_u.at[b], r_u.at[b])
        for k in range(7):
            sent(qown.at[b], s_q.at[b, k], r_q.at[b, k])
        sent(stash_in.at[0, b], s_ev.at[b], r_ev.at[b])
        sent(fwd_in.at[0], s_st.at[b], r_st.at[b])
        arrived(stash_out.at[0, b], s_st.at[b], r_st.at[b])
    for k in range(4):
        sent(weight.at[:, 0, 0], s_w.at[k], r_w.at[k])
    @pl.when(sec < nsec - 1)
    def _():
        sent(outb.at[0], s_next, r_next)

    @pl.when(sec > 0)
    def _():
        sent(outb.at[2], s_prev, r_prev)

    for k, out in enumerate((first_out, second_out, first_grad, second_grad)):
        near(outb.at[k], out.at[0], l_out.at[k]).wait()


def hand_over(*refs):
    for k in range(5):
        refs[5 + k][...] = refs[k][...]


def shards(nsec, fresh_in, fwd_in, fresh_cot, cot_in, stash_in, weight, gain):
    weight = weight.reshape(NZ, NY, 2, W, W)
    block = jax.ShapeDtypeStruct((1, TOK, W), BF)
    dma = pltpu.SemaphoreType.DMA
    vm = pltpu.VMEM
    scratch = [
        vm((4, NY, NZ, TOK, W), BF),
        vm((NY, NZ, W, 2 * W), BF),
        vm((1, NY * NZ * 2 * W), F32),
        vm((4, TOK, 2 * W + 128), F32),
        vm((4, TOK, W + 128), F32),
        vm((2, TOK, 2 * W), BF),
        vm((2, TOK, W), BF),
        vm((4, TOK, W), BF),
        vm((2, TOK, 128), F32),
        vm((2, NZ, TOK, W), BF),
        vm((2, NZ, TOK, W), BF),
        vm((2, NZ, 2, TOK, W), BF),
        vm((2, NZ, 2, TOK, W), BF),
        vm((2, NZ, TOK, W), BF),
        vm((2, NZ, TOK, W), BF),
        vm((TOK, W), F32),
        vm((2, 8, 128), F32),
        vm((2, 8, 128), F32),
        vm((2, NY, 8, 128), F32),
        vm((2, NZ, 8, 128), F32),
        vm((2, 2, 8, 128), F32),
        dma((4, NZ, 2)), dma((4, NZ)),
        dma((4, NZ, 2)), dma((4, NZ, 2)),
        dma((4, NZ, 2)), dma((4, NZ, 2)),
        dma((4,)), dma((4,)), dma((4,)),
        dma((4,)), dma((4,)), dma((2,)), dma((2,)),
        dma((2,)), dma((2,)), dma, dma, dma, dma, dma((2,)), dma((2,)),
        dma((5,)), dma((4,)),
        dma((2, NZ, 2)), dma((2, NZ, 2)), dma((2, NZ, 2)), dma((2, NZ, 2)),
        dma((2, NZ)), dma((2, NZ)),
        dma((2, 7)), dma((2, 7)),
    ]
    anywhere = pl.BlockSpec(memory_space=pl.ANY)
    outs = pl.pallas_call(
        functools.partial(kernel, nsec),
        out_shape=(block, block, block, block, jax.ShapeDtypeStruct((1, 2, TOK, W), BF)),
        in_specs=[anywhere] * 7,
        out_specs=(anywhere,) * 5,
        scratch_shapes=scratch,
        compiler_params=pltpu.CompilerParams(
            collective_id=0, has_side_effects=True, vmem_limit_bytes=56 * 2**20
        ),
        cost_estimate=pl.CostEstimate(flops=7_250_000_000, bytes_accessed=12_000_000, transcendentals=200_000),
    )(fresh_in, fwd_in, fresh_cot, cot_in, stash_in, weight, gain)
    return pl.pallas_call(
        hand_over,
        out_shape=tuple(jax.ShapeDtypeStruct(o.shape, o.dtype) for o in outs),
    )(*outs)


def solution(mesh):
    return jax.shard_map(
        functools.partial(shards, mesh.shape["section"]),
        mesh=mesh,
        in_specs=(
            P(None, "tp"),
            P("section", None, "tp"),
            P(None, "tp"),
            P("section", None, "tp"),
            P("section", None, None, "tp"),
            P("section", None, "tp"),
            P("section", None),
        ),
        out_specs=(
            P("section", None, "tp"),
            P("section", None, "tp"),
            P("section", None, "tp"),
            P("section", None, "tp"),
            P("section", None, None, "tp"),
        ),
        check_vma=False,
    )
```

```python
import functools

import jax
import jax.numpy as jnp
from jax import lax
from jax.experimental import pallas as pl
from jax.experimental.pallas import tpu as pltpu
from jax.sharding import PartitionSpec as P

EPS = 1e-05
GCOEF = 0.7978845608028654
MESH = pl.DeviceIdType.MESH

TOK = 128
W = 384
NZ = 4
NY = 4
HALF = TOK // 2
A, B, C, D = 0, 1, 2, 3
UNI = (A, C, D,)
BF = jnp.bfloat16
F32 = jnp.float32


def gelu_value(h):
    return 0.5 * h * (1.0 + jnp.tanh(GCOEF * (h + 0.044715 * h * h * h)))


def gelu_slope(h):
    tval = jnp.tanh(GCOEF * (h + 0.044715 * h * h * h))
    return 0.5 * (1.0 + tval) + 0.5 * h * (1.0 - tval * tval) * GCOEF * (
        1.0 + 3.0 * 0.044715 * h * h
    )


def kernel(
    nsec,
    fresh_in, fwd_in, fresh_cot, cot_in, stash_in, weight, gain,
    first_out, second_out, first_grad, second_grad, stash_out,
    xg, wc, gv, acc, hr, uu, cot, outb, rb,
    hsend, hin, fsend, fin, zsend, zin, dnacc, qown, qc, qy, qz, qsum,
    s_z, r_z, s_y, r_y, s_r, r_r,
    s_w, r_w, l_w,
    s_h, r_h, s_u, r_u,
    s_ev, r_ev, s_next, r_next, s_prev, r_prev, s_st, r_st,
    l_in, l_out,
    s_a, r_a, s_b, r_b, s_c, r_c,
    s_q, r_q,
):
    sec = lax.axis_index("section")
    tp = lax.axis_index("tp")
    core = lax.rem(tp, 2)
    y = lax.rem(tp // 2, NY)
    z = tp // (2 * NY)
    width = NZ * NY * 2 * W

    def at(zz, yy, cc=None):
        return (sec, (zz * NY + yy) * 2 + (core if cc is None else cc))

    def turn(v, k, n):
        return lax.rem(v + k, n)

    yr, yl, yo = turn(y, 1, NY), turn(y, 3, NY), turn(y, 2, NY)
    right, left, over = at(z, yr), at(z, yl), at(z, yo)
    twin = at(z, y, 1 - core)
    mirror = (nsec - 1 - sec, tp)
    after = (turn(sec, 1, nsec), tp)
    before = (turn(sec, nsec - 1, nsec), tp)

    def far(src, dst, ssem, rsem, dev):
        return pltpu.make_async_remote_copy(
            src_ref=src, dst_ref=dst, send_sem=ssem, recv_sem=rsem,
            device_id=dev, device_id_type=MESH,
        )

    def arrived(dst, ssem, rsem):
        far(dst, dst, ssem, rsem, twin).wait_recv()

    def sent(src, ssem, rsem):
        far(src, src, ssem, rsem, twin).wait_send()

    def near(src, dst, sem):
        return pltpu.make_async_copy(src, dst, sem)

    def local_in():
        near(fwd_in.at[0], xg.at[B, y, z], l_in.at[0]).start()
        near(gain, gv, l_in.at[1]).start()
        near(cot_in.at[0], cot.at[0], l_in.at[2]).start()

        @pl.when(sec == 0)
        def _():
            near(fresh_in, xg.at[D, y, z], l_in.at[3]).start()

        @pl.when(sec == nsec - 1)
        def _():
            near(fresh_cot, cot.at[1], l_in.at[4]).start()

        acc[...] = jnp.zeros_like(acc)

    for k, yy in enumerate((y, yl, yr, yo)):
        near(weight.at[:, yy, core], wc.at[yy, :, :, pl.ds(0, W)], l_w.at[k]).start()
    barrier = pltpu.get_barrier_semaphore()

    def greet(dev):
        pl.semaphore_signal(barrier, inc=1, device_id=dev, device_id_type=MESH)

    for k in range(1, NZ):
        greet(at(turn(z, k, NZ), y))
    for dev in (right, left, over, twin, mirror, after, before):
        greet(dev)
    local_in()
    pl.semaphore_wait(barrier, 10)

    below, above = at(turn(z, 3, NZ), y), at(turn(z, 1, NZ), y)

    def nearest(i):
        v = jnp.where((z == 0) | (z == 3), i, jnp.where(i < 2, 1 - i, i))
        return jnp.where(z < 2, v, 3 - v)

    def go_up(g, src, zq):
        far(src, xg.at[g, y, zq], s_z.at[g, zq, 0], r_z.at[g, zq], above).start()

    def go_down(g, src, zq):
        far(src, xg.at[g, y, zq], s_z.at[g, zq, 1], r_z.at[g, zq], below).start()

    def own_up(g, src):
        if g in UNI:
            for k in range(1, NZ):
                far(src, xg.at[g, y, z], s_z.at[g, k, 0], r_z.at[g, z],
                    at(turn(z, k, NZ), y)).start()
            return

        @pl.when(z < NZ - 1)
        def _():
            go_up(g, src, z)

        @pl.when(z > 0)
        def _():
            go_down(g, src, z)

    def own_across(g, src):
        far(src, xg.at[g, y, z], s_y.at[g, z, 0], r_y.at[g, z, 0], right).start()
        far(src, xg.at[g, y, z], s_y.at[g, z, 1], r_y.at[g, z, 1], left).start()

    def column_sends(g):
        def body(i, carry):
            zq = nearest(i)
            slot = xg.at[g, y, zq]
            arrived(slot, s_z.at[g, 0, 0], r_z.at[g, zq])

            if g not in UNI:
                @pl.when((zq < z) & (z < NZ - 1))
                def _():
                    go_up(g, slot, zq)

                @pl.when((zq > z) & (z > 0))
                def _():
                    go_down(g, slot, zq)

            far(slot, slot, s_y.at[g, zq, 0], r_y.at[g, zq, 0], right).start()
            far(slot, slot, s_y.at[g, zq, 1], r_y.at[g, zq, 1], left).start()
            return carry
        lax.fori_loop(1, NZ, body, 0)

    def product(g, yy, zq):
        x = xg[g, yy, zq].astype(F32)
        x2 = x * x
        acc[g, :, 2 * W:] += x2[:, :128] + x2[:, 128:256] + x2[:, 256:]
        start = pl.multiple_of(((zq * NY + yy) * 2 + core) * W, 128)
        n = (x * gv[:, pl.ds(start, W)]).astype(BF)
        acc[g, :, :2 * W] += jnp.dot(n, wc[yy, zq], preferred_element_type=F32)

    def relay(g):
        def body(i, carry):
            zq = nearest(i)
            from_left, from_right = xg.at[g, yl, zq], xg.at[g, yr, zq]
            arrived(from_left, s_z.at[g, 0, 0], r_y.at[g, zq, 0])
            top = from_left.at[pl.ds(0, HALF)]
            far(top, top, s_r.at[g, zq, 0], r_r.at[g, zq, 0], right).start()
            arrived(from_right, s_z.at[g, 0, 0], r_y.at[g, zq, 1])
            low = from_right.at[pl.ds(HALF, HALF)]
            far(low, low, s_r.at[g, zq, 1], r_r.at[g, zq, 1], left).start()
            product(g, y, zq)
            product(g, yl, zq)
            product(g, yr, zq)
            return carry
        lax.fori_loop(0, NZ, body, 0)

    def last_quarter(g):
        def body(i, carry):
            zq = nearest(i)
            slot = xg.at[g, yo, zq]
            arrived(slot.at[pl.ds(0, HALF)], s_z.at[g, 0, 0], r_r.at[g, zq, 0])
            arrived(slot.at[pl.ds(HALF, HALF)], s_z.at[g, 0, 0], r_r.at[g, zq, 1])
            product(g, yo, zq)
            return carry
        lax.fori_loop(0, NZ, body, 0)
        far(acc.at[g, :, pl.ds(W, W + 128)], hr.at[g], s_h.at[g], r_h.at[g], twin).start()

    def hidden(g):
        arrived(hr.at[g], s_z.at[g, 0, 0], r_h.at[g])
        ss = acc[g, :, 2 * W:] + hr[g, :, W:]
        radius = jnp.sqrt(jnp.sum(ss, axis=-1, keepdims=True) / width + EPS)
        h = (acc[g, :, :W] + hr[g, :, :W]) / radius
        return radius, h

    def part(b, yy, zq):
        return lax.dot_general(
            uu[b], wc[yy, zq], (((1,), (1,)), ((), ())), preferred_element_type=F32
        )

    def gradient_start(b, g):
        radius, h = hidden(g)
        u = (cot[b].astype(F32) * gelu_slope(h)).astype(BF)
        uu[b, :, :W] = u
        far(uu.at[b, :, pl.ds(0, W)], uu.at[b, :, pl.ds(W, W)], s_u.at[b], r_u.at[b], twin).start()
        rb[b] = jnp.broadcast_to(radius, (TOK, 128))
        e = u.astype(F32) * h
        lanes = (e[:, :128] + e[:, 128:256] + e[:, 256:]) * radius
        t = lanes.T
        q = t[0:8]
        for k in range(1, 16):
            q = q + t[8 * k:8 * k + 8]
        qown[b] = q
        far(qown.at[b], qc.at[b], s_q.at[b, 0], r_q.at[b, 0], twin).start()
        arrived(uu.at[b, :, pl.ds(W, W)], s_u.at[b], r_u.at[b])

    def scatter_over(b):
        def body(i, carry):
            zq = nearest(NZ - i)
            hsend[b, zq] = part(b, yo, zq).astype(BF)
            far(hsend.at[b, zq, pl.ds(0, HALF)], hin.at[b, zq, pl.ds(0, HALF)],
                s_a.at[b, zq, 0], r_a.at[b, zq, 0], right).start()
            far(hsend.at[b, zq, pl.ds(HALF, HALF)], hin.at[b, zq, pl.ds(HALF, HALF)],
                s_a.at[b, zq, 1], r_a.at[b, zq, 1], left).start()
            return carry
        lax.fori_loop(1, NZ + 1, body, 0)

    def scatter_sides(b):
        arrived(qc.at[b], s_q.at[b, 0], r_q.at[b, 0])
        qsum[b, 0] = qown[b] + qc[b]
        for k in range(1, NY):
            far(qsum.at[b, 0], qy.at[b, k], s_q.at[b, k], r_q.at[b, k],
                at(z, turn(y, k, NY))).start()

        def body(i, carry):
            zq = nearest(NZ - i)
            to_right = part(b, yr, zq)
            arrived(hin.at[b, zq, pl.ds(0, HALF)], s_a.at[b, zq, 0], r_a.at[b, zq, 0])
            fsend[b, zq, 0, :HALF] = (to_right[:HALF] + hin[b, zq, :HALF].astype(F32)).astype(BF)
            fsend[b, zq, 0, HALF:] = to_right[HALF:].astype(BF)
            far(fsend.at[b, zq, 0], fin.at[b, zq, 0], s_b.at[b, zq, 0], r_b.at[b, zq, 0], right).start()
            to_left = part(b, yl, zq)
            arrived(hin.at[b, zq, pl.ds(HALF, HALF)], s_a.at[b, zq, 1], r_a.at[b, zq, 1])
            fsend[b, zq, 1, :HALF] = to_left[:HALF].astype(BF)
            fsend[b, zq, 1, HALF:] = (to_left[HALF:] + hin[b, zq, HALF:].astype(F32)).astype(BF)
            far(fsend.at[b, zq, 1], fin.at[b, zq, 1], s_b.at[b, zq, 1], r_b.at[b, zq, 1], left).start()
            return carry
        lax.fori_loop(1, NZ + 1, body, 0)

    def own_column(b, zq):
        mine = part(b, y, zq)
        arrived(fin.at[b, zq, 0], s_b.at[b, zq, 0], r_b.at[b, zq, 0])
        arrived(fin.at[b, zq, 1], s_b.at[b, zq, 1], r_b.at[b, zq, 1])
        return mine + fin[b, zq, 0].astype(F32) + fin[b, zq, 1].astype(F32)

    def scatter_column(b):
        total = qsum[b, 0]
        for k in range(1, NY):
            arrived(qy.at[b, k], s_q.at[b, k], r_q.at[b, k])
            total = total + qy[b, k]
        qsum[b, 1] = total
        for k in range(1, NZ):
            far(qsum.at[b, 1], qz.at[b, k], s_q.at[b, 3 + k], r_q.at[b, 3 + k],
                at(turn(z, k, NZ), y)).start()

        def body(i, carry):
            zq = nearest(NZ - i)
            zsend[b, zq] = own_column(b, zq).astype(BF)
            far(zsend.at[b, zq], zin.at[b, z], s_c.at[b, zq], r_c.at[b, z], at(zq, y)).start()
            return carry
        lax.fori_loop(1, NZ, body, 0)
        dnacc[...] = own_column(b, z)

    def gradient_end(b, g):
        total = qsum[b, 1]
        for k in range(1, NZ):
            arrived(qz.at[b, k], s_q.at[b, 3 + k], r_q.at[b, 3 + k])
            total = total + qz[b, k]
        row = jnp.sum(total, axis=0, keepdims=True)
        inner = jnp.broadcast_to(row, (128, TOK)).T[:, :1]
        dn = dnacc[...]
        for k in range(1, NZ):
            zq = turn(z, k, NZ)
            arrived(zin.at[b, zq], s_c.at[b, zq], r_c.at[b, zq])
            dn = dn + zin[b, zq].astype(F32)
        radius = rb[b][:, :1]
        mine = pl.multiple_of(tp * W, 128)
        x = xg[g, y, z].astype(F32)
        grad = (
            cot[b].astype(F32)
            + gv[:, pl.ds(mine, W)] * dn / radius
            - x * (inner / (width * radius * radius * radius))
        )
        outb[2 + b] = grad.astype(BF)

    def forward_end(g, slot):
        radius, h = hidden(g)
        outb[slot] = (xg[g, y, z].astype(F32) + gelu_value(h)).astype(BF)

    def mine(g):
        return xg.at[g, y, z]

    def weight_in():
        for k, yy in enumerate((y, yl, yr, yo)):
            far(weight.at[:, yy, 1 - core], wc.at[yy, :, :, pl.ds(W, W)], s_w.at[k], r_w.at[k], twin).start()

    def small_wait():
        near(fwd_in.at[0], mine(B), l_in.at[0]).wait()
        near(gain, gv, l_in.at[1]).wait()
        near(cot_in.at[0], cot.at[0], l_in.at[2]).wait()

    def weight_wait(quarters):
        for k, yy in quarters:
            near(weight.at[:, yy, core], wc.at[yy, :, :, pl.ds(0, W)], l_w.at[k]).wait()
            arrived(wc.at[yy, :, :, pl.ds(W, W)], s_w.at[k], r_w.at[k])

    def saved_in(b, g):
        far(stash_in.at[0, b], mine(g), s_ev.at[b], r_ev.at[b], mirror).start()

    def saved_wait(b, g):
        arrived(mine(g), s_ev.at[b], r_ev.at[b])

    def stash_first():
        far(mine(B), stash_out.at[0, 0], s_st.at[0], r_st.at[0], mirror).start()

    def stash_second():
        far(mine(D), stash_out.at[0, 1], s_st.at[1], r_st.at[1], mirror).start()

    def next_in():
        @pl.when(sec < nsec - 1)
        def _():
            far(outb.at[0], mine(D), s_next, r_next, after).start()

        near(outb.at[0], first_out.at[0], l_out.at[0]).start()

    def next_wait():
        @pl.when(sec == 0)
        def _():
            near(fresh_in, mine(D), l_in.at[3]).wait()

        @pl.when(sec > 0)
        def _():
            arrived(mine(D), s_next, r_next)

    def cot_out():
        @pl.when(sec > 0)
        def _():
            far(outb.at[2], cot.at[1], s_prev, r_prev, before).start()

        near(outb.at[2], first_grad.at[0], l_out.at[2]).start()

    def cot_wait():
        @pl.when(sec == nsec - 1)
        def _():
            near(fresh_cot, cot.at[1], l_in.at[4]).wait()

        @pl.when(sec < nsec - 1)
        def _():
            arrived(cot.at[1], s_prev, r_prev)

    def second_done():
        near(outb.at[1], second_out.at[0], l_out.at[1]).start()

    def grad_done():
        near(outb.at[3], second_grad.at[0], l_out.at[3]).start()

    saved_in(0, A)
    own_up(B, fwd_in.at[0])
    own_across(B, fwd_in.at[0])
    weight_in()
    column_sends(B)
    small_wait()
    saved_wait(0, A)
    own_up(A, mine(A))
    own_across(A, mine(A))
    saved_in(1, C)
    weight_wait(((0, y), (1, yl), (2, yr)))
    relay(B)
    column_sends(A)
    weight_wait(((3, yo),))
    last_quarter(B)
    forward_end(B, 0)
    next_in()
    relay(A)
    saved_wait(1, C)
    own_up(C, mine(C))
    last_quarter(A)
    own_across(C, mine(C))
    next_wait()
    own_up(D, mine(D))
    gradient_start(0, A)
    scatter_over(0)
    scatter_sides(0)
    column_sends(C)
    stash_first()
    scatter_column(0)
    relay(C)
    own_across(D, mine(D))
    column_sends(D)
    gradient_end(0, A)
    cot_out()
    last_quarter(C)
    stash_second()
    cot_wait()
    gradient_start(1, C)
    scatter_over(1)
    relay(D)
    scatter_sides(1)
    last_quarter(D)
    scatter_column(1)
    forward_end(D, 1)
    second_done()
    gradient_end(1, C)
    grad_done()

    for g in range(4):
        if g in UNI:
            for k in range(1, NZ):
                sent(xg.at[g, y, z], s_z.at[g, k, 0], r_z.at[g, z])

        def sends_of(i, carry):
            slot = xg.at[g, 0, i]

            if g not in UNI:
                @pl.when((i <= z) & (z < NZ - 1))
                def _():
                    sent(slot, s_z.at[g, i, 0], r_z.at[g, i])

                @pl.when((i >= z) & (z > 0))
                def _():
                    sent(slot, s_z.at[g, i, 1], r_z.at[g, i])

            half = slot.at[pl.ds(0, HALF)]
            for k in range(2):
                sent(slot, s_y.at[g, i, k], r_y.at[g, i, k])
                sent(half, s_r.at[g, i, k], r_r.at[g, i, k])
            return carry
        lax.fori_loop(0, NZ, sends_of, 0)
        sent(acc.at[g, :, pl.ds(W, W + 128)], s_h.at[g], r_h.at[g])
    for b in range(2):
        def sends_to(i, carry):
            for k in range(2):
                sent(hsend.at[b, i, pl.ds(0, HALF)], s_a.at[b, i, k], r_a.at[b, i, k])
                sent(fsend.at[b, i, k], s_b.at[b, i, k], r_b.at[b, i, k])
            return carry
        lax.fori_loop(0, NZ, sends_to, 0)

        def sends_up(i, carry):
            zq = turn(z, i, NZ)
            sent(zsend.at[b, zq], s_c.at[b, zq], r_c.at[b, zq])
            return carry
        lax.fori_loop(1, NZ, sends_up, 0)
        sent(uu.at[b, :, pl.ds(0, W)], s_u.at[b], r_u.at[b])
        for k in range(7):
            sent(qown.at[b], s_q.at[b, k], r_q.at[b, k])
        sent(stash_in.at[0, b], s_ev.at[b], r_ev.at[b])
        sent(fwd_in.at[0], s_st.at[b], r_st.at[b])
        arrived(stash_out.at[0, b], s_st.at[b], r_st.at[b])
    for k in range(4):
        sent(weight.at[:, 0, 0], s_w.at[k], r_w.at[k])
    @pl.when(sec < nsec - 1)
    def _():
        sent(outb.at[0], s_next, r_next)

    @pl.when(sec > 0)
    def _():
        sent(outb.at[2], s_prev, r_prev)

    for k, out in enumerate((first_out, second_out, first_grad, second_grad)):
        near(outb.at[k], out.at[0], l_out.at[k]).wait()


def hand_over(*refs):
    for k in range(5):
        refs[5 + k][...] = refs[k][...]


def shards(nsec, fresh_in, fwd_in, fresh_cot, cot_in, stash_in, weight, gain):
    weight = weight.reshape(NZ, NY, 2, W, W)
    block = jax.ShapeDtypeStruct((1, TOK, W), BF)
    dma = pltpu.SemaphoreType.DMA
    vm = pltpu.VMEM
    scratch = [
        vm((4, NY, NZ, TOK, W), BF),
        vm((NY, NZ, W, 2 * W), BF),
        vm((1, NY * NZ * 2 * W), F32),
        vm((4, TOK, 2 * W + 128), F32),
        vm((4, TOK, W + 128), F32),
        vm((2, TOK, 2 * W), BF),
        vm((2, TOK, W), BF),
        vm((4, TOK, W), BF),
        vm((2, TOK, 128), F32),
        vm((2, NZ, TOK, W), BF),
        vm((2, NZ, TOK, W), BF),
        vm((2, NZ, 2, TOK, W), BF),
        vm((2, NZ, 2, TOK, W), BF),
        vm((2, NZ, TOK, W), BF),
        vm((2, NZ, TOK, W), BF),
        vm((TOK, W), F32),
        vm((2, 8, 128), F32),
        vm((2, 8, 128), F32),
        vm((2, NY, 8, 128), F32),
        vm((2, NZ, 8, 128), F32),
        vm((2, 2, 8, 128), F32),
        dma((4, NZ, 2)), dma((4, NZ)),
        dma((4, NZ, 2)), dma((4, NZ, 2)),
        dma((4, NZ, 2)), dma((4, NZ, 2)),
        dma((4,)), dma((4,)), dma((4,)),
        dma((4,)), dma((4,)), dma((2,)), dma((2,)),
        dma((2,)), dma((2,)), dma, dma, dma, dma, dma((2,)), dma((2,)),
        dma((5,)), dma((4,)),
        dma((2, NZ, 2)), dma((2, NZ, 2)), dma((2, NZ, 2)), dma((2, NZ, 2)),
        dma((2, NZ)), dma((2, NZ)),
        dma((2, 7)), dma((2, 7)),
    ]
    anywhere = pl.BlockSpec(memory_space=pl.ANY)
    outs = pl.pallas_call(
        functools.partial(kernel, nsec),
        out_shape=(block, block, block, block, jax.ShapeDtypeStruct((1, 2, TOK, W), BF)),
        in_specs=[anywhere] * 7,
        out_specs=(anywhere,) * 5,
        scratch_shapes=scratch,
        compiler_params=pltpu.CompilerParams(
            collective_id=0, has_side_effects=True, vmem_limit_bytes=56 * 2**20
        ),
        cost_estimate=pl.CostEstimate(flops=7_250_000_000, bytes_accessed=12_000_000, transcendentals=200_000),
    )(fresh_in, fwd_in, fresh_cot, cot_in, stash_in, weight, gain)
    return pl.pallas_call(
        hand_over,
        out_shape=tuple(jax.ShapeDtypeStruct(o.shape, o.dtype) for o in outs),
    )(*outs)


def solution(mesh):
    return jax.shard_map(
        functools.partial(shards, mesh.shape["section"]),
        mesh=mesh,
        in_specs=(
            P(None, "tp"),
            P("section", None, "tp"),
            P(None, "tp"),
            P("section", None, "tp"),
            P("section", None, None, "tp"),
            P("section", None, "tp"),
            P("section", None),
        ),
        out_specs=(
            P("section", None, "tp"),
            P("section", None, "tp"),
            P("section", None, "tp"),
            P("section", None, "tp"),
            P("section", None, None, "tp"),
        ),
        check_vma=False,
    )
```
